32 devices in a mesh: sec: 2 (over core), dp: 4 (over y, x), tp: 4 (over z).
Axes of the slice: x: 2, y: 2, z: 4, core: 2. Of those that a mesh axis runs over, the one named last changes fastest.
Arguments:
- feats: bfloat16 [2, 512, 1280], P('sec', 'dp'), may hold values from -6 to 6
- dest: int32 [2, 512, 1], P('sec', 'dp'), may hold values from 0 to 3; in each aligned block of 128 rows (0 to 127, 128 to 255, ..., all dimensions but the last counted through in order) at most 64 rows name the same one
- proj_w: bfloat16 [1280, 8192], P(('sec', 'dp'), 'tp'), may hold values from -0.15625 to 0.15625
- proj_b: bfloat16 [8192], P('tp'), may hold values from -3 to 3
- text: bfloat16 [2, 1024, 8192], P('sec', 'dp', 'tp'), may hold values from -6 to 6
- gain: bfloat16 [8192], P('tp'), may hold values from 0.5 to 1.5
- cot: bfloat16 [2, 1024, 8192], P('sec', 'dp', 'tp'), may hold values from -6 to 6
Outputs:
- normed: bfloat16 [2, 1024, 8192], P('sec', 'dp', 'tp')
- feature_grad: bfloat16 [2, 512, 1280], P('sec', 'dp')
The draws below stay inside these ranges and needn't reach their ends.
Inputs may be any that keep to these rules, and one draw needn't show every extreme that they name: `dest`: among the 128 tokens of one dp index in one micro-batch, no target is named more than 64 times, a bound that some block reaches.
All inputs are finite; a program needn't handle non-finite values.
Results may differ from the reference program's by a relative error of at most 0.005.
Values may be sent and summed in bfloat16 or wider, within the bound.
A program may use at most 64 MiB of HBM per device.

```python
import math
import jax
import jax.numpy as jnp
import numpy as np
from jax import lax

D = 8192
VD = 1280
IMG = 128
CAP = 64
ROWS = 256
TOK = 512
LLM_ROWS = 1024
N_SEC = 2
N_DP = 4


def level_of(rng, dims, cuts, low, top_value):
    def one(dim, parts):
        draws = jax.random.uniform(jax.random.fold_in(jax.random.fold_in(rng, 6), dim), (parts,), jnp.float32, low / len(cuts), top_value / len(cuts))
        return jnp.repeat(jnp.exp(draws), dims[dim] // parts).reshape((-1,) + (1,) * (len(dims) - dim - 1))

    loudness = one(*cuts[0])
    for cut in cuts[1:]:
        loudness = loudness * one(*cut)
    return loudness


def shared_out(rng, own, number, rows, amount, top, limit, lean):
    ranking = jax.random.permutation(rng, amount)
    crowded, ordinary = load_shares(amount, rows * top, limit, lean, True), load_shares(amount, rows * top, limit, lean, False)
    places = jnp.arange(amount)

    def named(sizes, turn):
        used = int((sizes > 0).sum())
        fixed = max(1, used // 4)
        moved = fixed + (places - fixed + turn * (used - fixed)) % max(1, amount - fixed)
        return jnp.zeros((amount,), jnp.int32).at[ranking[jnp.where(places < fixed, places, moved)]].set(jnp.asarray(sizes, jnp.int32))

    sizes = jnp.where(number % 4 == 0, named(crowded, number // 4), named(ordinary, number - number // 4 - 1))
    mixed = jax.random.permutation(jax.random.fold_in(own, 3), amount)
    source_of, sink = mixed[0:amount // 2 * 2:2], mixed[1:amount // 2 * 2:2]
    room = jnp.minimum(sizes[source_of] - 1, limit - sizes[sink]) // 2
    room = jnp.where((source_of == ranking[0]) | (sink == ranking[0]) | (sizes[sink] == 0), 0, jnp.maximum(room, 0))
    moved = jax.random.randint(jax.random.fold_in(own, 4), (amount // 2,), 0, 1 << 20) % (room + 1)
    sizes = sizes.at[source_of].add(-moved).at[sink].add(moved)
    members = jnp.searchsorted(jnp.cumsum(sizes), jnp.arange(rows * top), side="right").astype(jnp.int32)
    grid = members.reshape(top, rows).T
    grid = grid[jax.random.permutation(jax.random.fold_in(own, 1), rows)]
    turn = jax.random.randint(jax.random.fold_in(own, 2), (rows, 1), 0, top)
    return jnp.take_along_axis(grid, (jnp.arange(top)[None, :] + turn) % top, axis=1)


def load_shares(number_of, total, bound, slope, full):
    loads = [(1 << 20) // math.isqrt(grade ** slope) + 1 for grade in range(1, number_of + 1)]
    largest = bound if full else min(bound, max(-(-total // number_of), total * loads[0] // sum(loads)))
    least = 1 if total - largest >= number_of - 1 else 0
    counts, surplus = [largest] + [least] * (number_of - 1), total - largest - least * (number_of - 1)
    while surplus > 0:
        free = [i for i in range(1, number_of) if counts[i] < largest] or [i for i in range(1, number_of) if counts[i] < bound]
        pool, left = sum([loads[i] for i in free]), surplus
        for i in free:
            extra = min(bound - counts[i], max(1, left * loads[i] // pool), surplus)
            counts[i] = counts[i] + extra
            surplus = surplus - extra
    return np.array(counts)


def normal_values(key, extent, scale, bound, pieces=(), held_as=jnp.bfloat16):
    values = jax.random.normal(key, extent, jnp.float32) * scale
    if len(pieces) > 0:
        values = level_of(key, extent, pieces, -0.22, 0.18) * values
    return jnp.clip(values, min=-bound, max=bound).astype(held_as)


def setup_inputs(seed: int = 0) -> dict:
    streams_of = jax.random.split(jax.random.key(seed), 8)
    feats = normal_values(streams_of[0], (N_SEC, TOK, VD), 1.0, 6.0, ((0, 2), (1, 4)))
    dest_keys = jax.random.split(jax.random.fold_in(streams_of[1], 1), N_SEC * TOK // IMG)
    dest_turns = jax.random.permutation(jax.random.fold_in(streams_of[1], 3), N_SEC * TOK // IMG)
    dest = jax.vmap(lambda own, number: shared_out(jax.random.fold_in(streams_of[1], 2), own, number, IMG, N_DP, 1, CAP, 2))(dest_keys, dest_turns).reshape((N_SEC, TOK, 1))
    proj_w = normal_values(streams_of[2], (VD, D), VD ** -0.5, 0.15625, ((0, 8), (1, 4)))
    proj_b = normal_values(streams_of[3], (D,), 0.5, 3.0, ((0, 4),))
    text = normal_values(streams_of[4], (N_SEC, LLM_ROWS, D), 1.0, 6.0, ((0, 2), (1, 4), (2, 4)))
    gain = jnp.clip(1.0 + 0.1 * jax.random.normal(streams_of[5], (D,), jnp.float32), 0.5, 1.5).astype(jnp.bfloat16)
    cot = normal_values(streams_of[6], (N_SEC, LLM_ROWS, D), 1.0, 6.0, ((0, 2), (1, 4), (2, 4)))
    return dict(feats=feats, dest=dest, proj_w=proj_w, proj_b=proj_b, text=text, gain=gain, cot=cot)


def reference(feats, dest, proj_w, proj_b, text, gain, cot):
    lanes = jnp.arange(N_DP, dtype=jnp.int32)
    source = jnp.arange(N_DP, dtype=jnp.int32)[:, None]
    normed_list = [None] * N_SEC
    grad_list = [None] * N_SEC
    gain_wide = gain.astype(jnp.float32)
    for micro in range(N_SEC):
        segment = (micro + 1) % N_SEC
        target = dest[micro, :, 0].reshape(N_DP, IMG).astype(jnp.int32)
        onehot = (target[:, :, None] == lanes[None, None, :]).astype(jnp.int32)
        before = jnp.cumsum(onehot, axis=1) - onehot
        position = lax.optimization_barrier(jnp.sum(before * onehot, axis=-1)).astype(jnp.int32)
        row_index = (target * ROWS + source * CAP + position).reshape(-1).astype(jnp.int32)
        projected = (jnp.dot(feats[micro], proj_w, preferred_element_type=jnp.float32) + proj_b.astype(jnp.float32)).astype(jnp.bfloat16)
        packed = jnp.zeros((N_DP * ROWS, D), jnp.float32).at[row_index].set(projected.astype(jnp.float32))
        filled = jnp.zeros((N_DP * ROWS,), jnp.float32).at[row_index].set(1.0)
        hidden = jnp.where(filled[:, None] > 0.5, packed, text[segment].astype(jnp.float32))
        inverse = jax.lax.rsqrt(lax.optimization_barrier(jnp.mean(hidden * hidden, axis=-1)) + 1e-05)
        normed = (hidden * inverse[:, None] * gain_wide).astype(jnp.bfloat16)
        scaled = cot[segment].astype(jnp.float32) * gain_wide
        cross = lax.optimization_barrier(jnp.mean(scaled * hidden, axis=-1))
        grad_hidden = (inverse[:, None] * scaled - hidden * (inverse * inverse * inverse * cross)[:, None]).astype(jnp.bfloat16)
        grad_tokens = grad_hidden[row_index]
        feature_grad = jnp.dot(grad_tokens, proj_w.T, preferred_element_type=jnp.float32).astype(jnp.bfloat16)
        normed_list[segment] = normed
        grad_list[micro] = feature_grad
    return (jnp.stack(normed_list), jnp.stack(grad_list))
```

```python
import functools

import jax
import jax.numpy as jnp
from jax import lax
from jax.experimental import pallas as pl
from jax.experimental.pallas import tpu as pltpu
from jax.sharding import PartitionSpec as P


def from_behind(value, axis, steps):
    count = lax.axis_size(axis)
    pairs = [(source, (source + steps) % count) for source in range(count)]
    return lax.ppermute(value, axis, pairs)


def route_forward(outgoing):
    regrouped = lax.all_to_all(outgoing, "dp", split_axis=0, concat_axis=0, tiled=True)
    return from_behind(regrouped, "sec", 1)


def route_backward(incoming):
    hopped = from_behind(incoming, "sec", -1)
    return lax.all_to_all(hopped, "dp", split_axis=0, concat_axis=0, tiled=True)


def body(feats, dest, proj_w, proj_b, text, gain, cot):
    rows_in = feats[0]
    per_device = rows_in.shape[0]
    group_size = lax.axis_size("dp")
    tp_size = lax.axis_size("tp")
    capacity = 2 * per_device // group_size
    slot_total = group_size * capacity
    weight = lax.all_gather(proj_w, ("sec", "dp"), axis=0, tiled=True)
    target = dest[0, :, 0]
    lanes = jnp.arange(group_size, dtype=jnp.int32)
    onehot = (target[:, None] == lanes[None, :]).astype(jnp.int32)
    before = jnp.cumsum(onehot, axis=0) - onehot
    position = jnp.sum(before * onehot, axis=1)
    slot_index = target * capacity + position
    placer = (jnp.arange(slot_total, dtype=jnp.int32)[:, None] == slot_index[None, :]).astype(
        jnp.bfloat16
    )
    bias_wide = proj_b.astype(jnp.float32)
    counts = jnp.sum(onehot, axis=0).reshape(group_size, 1)
    counts_moved = lax.all_to_all(counts, "dp", split_axis=0, concat_axis=0, tiled=True)
    counts_in = from_behind(counts_moved, "sec", 1)
    occupied = (jnp.arange(capacity, dtype=jnp.int32)[None, :] < counts_in).reshape(slot_total, 1)
    projected = (jnp.dot(rows_in, weight, preferred_element_type=jnp.float32) + bias_wide).astype(
        jnp.bfloat16
    )
    outgoing = jnp.dot(placer, projected, preferred_element_type=jnp.float32).astype(jnp.bfloat16)
    arrived = route_forward(outgoing.reshape(group_size, capacity, -1))
    packed = arrived.reshape(slot_total, -1)
    gain_wide = gain.astype(jnp.float32)
    hidden = jnp.where(occupied, packed.astype(jnp.float32), text[0].astype(jnp.float32))
    scaled = cot[0].astype(jnp.float32) * gain_wide
    squares, cross = lax.psum(
        (jnp.sum(hidden * hidden, axis=1), jnp.sum(scaled * hidden, axis=1)), "tp"
    )
    full_width = hidden.shape[1] * tp_size
    inverse = lax.rsqrt(squares / full_width + 1e-05)
    normed = (hidden * inverse[:, None] * gain_wide).astype(jnp.bfloat16)
    grad_hidden = (
        inverse[:, None] * scaled
        - hidden * (inverse * inverse * inverse * cross / full_width)[:, None]
    ).astype(jnp.bfloat16)
    returned = route_backward(grad_hidden.reshape(group_size, capacity, -1)).reshape(slot_total, -1)
    grad_tokens = jnp.dot(placer.T, returned, preferred_element_type=jnp.float32).astype(
        jnp.bfloat16
    )
    partial_value = lax.dot_general(
        grad_tokens, weight, (((1,), (1,)), ((), ())), preferred_element_type=jnp.float32
    )
    feature_grad = lax.psum(partial_value, "tp").astype(jnp.bfloat16)
    return (normed[None], feature_grad[None])


MESH = pl.DeviceIdType.MESH
FLAG = 128
CHUNKS = 8
AHEAD = 3
PARTS = 5


def kernel(
    feats_ref, dest_ref, shard_ref, bias_ref, text_hbm, gain_ref, cot_hbm,
    normed_ref, grad_ref,
    weight, text, cot, outbox, slots, hidden, grad, product, returned, tokens, partial, result, stats,
    local_sem, w_send, w_recv, x_send, x_recv, y_send, y_recv, s_send, s_recv,
    p_send, p_recv, r_send, r_recv, g_send, g_recv,
):
    sec, dp, tp = lax.axis_index("sec"), lax.axis_index("dp"), lax.axis_index("tp")
    other = 1 - sec
    x_dp = dp + 1 - 2 * lax.rem(dp, 2)
    y_dp = lax.rem(dp + 2, 4)
    d_dp = 3 - dp
    per_device, vision = feats_ref.shape
    depth, width = shard_ref.shape
    n_dp, n_tp, quarter, _ = slots.shape
    cap = n_tp * quarter
    rows = n_dp * cap
    cw = width // CHUNKS
    pw = vision // PARTS
    tok_q = per_device // n_tp
    half = depth // 2

    def block(sec_of, dp_of):
        return pl.multiple_of((sec_of * n_dp + dp_of) * depth, 16)

    own = block(sec, dp)
    local = [
        pltpu.make_async_copy(shard_ref, weight.at[pl.ds(own, depth)], local_sem.at[0]),
        pltpu.make_async_copy(text_hbm, text, local_sem.at[1]),
        pltpu.make_async_copy(cot_hbm, cot, local_sem.at[2]),
    ]
    for copy in local:
        copy.start()

    barrier = pltpu.get_barrier_semaphore()
    peers = [(sec, x_dp, tp), (sec, y_dp, tp), (sec, d_dp, tp)]
    peers += [(other, dp, tp), (other, x_dp, tp), (other, y_dp, tp), (other, d_dp, tp)]
    peers += [(sec, dp, lax.rem(tp + k, n_tp)) for k in range(1, n_tp)]
    for peer in peers:
        pl.semaphore_signal(barrier, inc=1, device_id=peer, device_id_type=MESH)

    t_col = dest_ref[...].astype(jnp.float32)
    square = (per_device, per_device)
    down = lax.broadcasted_iota(jnp.int32, square, 0)
    along = lax.broadcasted_iota(jnp.int32, square, 1)
    t_row = jnp.sum(jnp.where(down == along, t_col, 0.0), axis=0, keepdims=True)
    same = t_col == t_row
    before_row = jnp.sum(jnp.where(same & (down < along), 1.0, 0.0), axis=0, keepdims=True)
    before_col = jnp.sum(jnp.where(same & (along < down), 1.0, 0.0), axis=1, keepdims=True)
    slot_row = (t_row * cap + before_row).astype(jnp.int32)
    slot_col = (t_col * cap + before_col).astype(jnp.int32)
    mine = lax.broadcasted_iota(jnp.int32, (n_dp * quarter, per_device), 0)
    mine = mine + (mine // quarter) * (cap - quarter) + tp * quarter
    placer = jnp.where(mine == slot_row, 1.0, 0.0)
    filled = jnp.broadcast_to(jnp.sum(placer, axis=1, keepdims=True), (n_dp * quarter, FLAG))
    routed = jnp.dot(placer.astype(jnp.bfloat16), feats_ref[...], preferred_element_type=jnp.float32)
    outbox[:, :, pl.ds(0, vision)] = routed.astype(jnp.bfloat16).reshape(n_dp, quarter, vision)
    outbox[:, :, pl.ds(vision, FLAG)] = filled.astype(jnp.bfloat16).reshape(n_dp, quarter, FLAG)
    unplacer = jnp.where(
        slot_col == lax.broadcasted_iota(jnp.int32, (per_device, rows), 1), 1.0, 0.0
    ).astype(jnp.bfloat16)

    def remote(src, dst, send, recv, device):
        return pltpu.make_async_remote_copy(
            src_ref=src, dst_ref=dst, send_sem=send, recv_sem=recv,
            device_id=device, device_id_type=MESH,
        )

    sent = []

    def start(copy):
        copy.start()
        sent.append(copy)

    def w_copy(first, count, chunk, kind, device):
        ref = weight.at[pl.ds(first, count), pl.ds(chunk * cw, cw)]
        return remote(ref, ref, w_send.at[chunk, kind], w_recv.at[chunk, kind], device)

    to_x, to_y, to_sib = (sec, x_dp, tp), (sec, y_dp, tp), (other, dp, tp)
    jx, jy, jd = block(sec, x_dp), block(sec, y_dp), block(sec, d_dp)
    jd_low = pl.multiple_of(jd + half, 16)
    jy_low = pl.multiple_of(jy + half, 16)
    sib = [block(other, k) for k in (dp, x_dp, y_dp, d_dp)]

    def send_own(chunk):
        start(w_copy(own, depth, chunk, 0, to_x))
        start(w_copy(own, depth, chunk, 1, to_y))
        start(w_copy(own, depth, chunk, 4, to_sib))

    local[0].wait()
    pl.semaphore_wait(barrier, len(peers))

    for to in (d_dp, x_dp, y_dp, dp):
        start(remote(outbox.at[to], slots.at[dp, tp], x_send.at[to], x_recv.at[dp], (other, to, tp)))
    for chunk in range(AHEAD):
        send_own(chunk)
    for source in range(n_dp):
        remote(outbox.at[source], slots.at[source, tp], x_send.at[source], x_recv.at[source], to_sib).wait_recv()
    for k in range(1, n_tp):
        to = lax.rem(tp + k, n_tp)
        start(remote(slots.at[:, tp], slots.at[:, tp], y_send.at[k], y_recv.at[tp], (sec, dp, to)))

    def project(chunk, square_sum, cross_sum):
        cols = pl.ds(chunk * cw, cw)
        value = jnp.dot(
            slots[:, :, :, pl.ds(0, vision)].reshape(rows, vision),
            weight[:, cols],
            preferred_element_type=jnp.float32,
        )
        value = (value + bias_ref[:, cols].astype(jnp.float32)).astype(jnp.bfloat16)
        flag = slots[:, :, :, pl.ds(vision, FLAG)].reshape(rows, FLAG).astype(jnp.float32)
        flag = jnp.concatenate([flag] * (cw // FLAG), axis=1)
        hid = jnp.where(flag > 0.5, value.astype(jnp.float32), text[:, cols].astype(jnp.float32))
        hidden[:, cols] = hid.astype(jnp.bfloat16)
        scaled = cot[:, cols].astype(jnp.float32) * gain_ref[:, cols].astype(jnp.float32)
        for first in range(0, cw, 128):
            part = hid[:, first:first + 128]
            square_sum = square_sum + part * part
            cross_sum = cross_sum + part * scaled[:, first:first + 128]
        return square_sum, cross_sum

    square_sum = jnp.zeros((rows, 128), jnp.float32)
    cross_sum = jnp.zeros((rows, 128), jnp.float32)
    for step in range(CHUNKS + 2):
        if step < CHUNKS:
            w_copy(jx, depth, step, 0, to_x).wait_recv()
            start(w_copy(jx, half, step, 2, to_y))
            w_copy(jy, depth, step, 1, to_y).wait_recv()
            start(w_copy(jy_low, half, step, 3, to_x))
            start(w_copy(jx, depth, step, 5, to_sib))
            start(w_copy(jy, depth, step, 6, to_sib))
            if step + AHEAD < CHUNKS:
                send_own(step + AHEAD)
        if 1 <= step <= CHUNKS:
            w_copy(jd, half, step - 1, 2, to_y).wait_recv()
            w_copy(jd_low, half, step - 1, 3, to_x).wait_recv()
            start(w_copy(jd, depth, step - 1, 7, to_sib))
        if step == 2:
            for k in range(1, n_tp):
                who = lax.rem(tp + k, n_tp)
                remote(slots.at[:, who], slots.at[:, who], y_send.at[k], y_recv.at[who], to_sib).wait_recv()
            local[1].wait()
            local[2].wait()
        if step >= 2:
            for kind in range(4):
                w_copy(sib[kind], depth, step - 2, 4 + kind, to_sib).wait_recv()
            square_sum, cross_sum = project(step - 2, square_sum, cross_sum)

    stats[tp, pl.ds(0, 1), :] = jnp.sum(square_sum.T, axis=0, keepdims=True)
    stats[tp, pl.ds(1, 1), :] = jnp.sum(cross_sum.T, axis=0, keepdims=True)
    for k in range(1, n_tp):
        to = lax.rem(tp + k, n_tp)
        start(remote(stats.at[tp], stats.at[tp], s_send.at[k], s_recv.at[tp], (sec, dp, to)))
    for k in range(1, n_tp):
        who = lax.rem(tp + k, n_tp)
        remote(stats.at[who], stats.at[who], s_send.at[k], s_recv.at[who], to_sib).wait_recv()
    total = stats[0] + stats[1] + stats[2] + stats[3]
    full_width = width * n_tp
    inverse = lax.rsqrt(total[0:1] / full_width + 1e-05)
    factor = inverse * inverse * inverse * total[1:2] / full_width
    inverse = jnp.broadcast_to(inverse, (128, rows)).T
    factor = jnp.broadcast_to(factor, (128, rows)).T
    inverse_wide = jnp.concatenate([inverse] * (cw // 128), axis=1)
    factor_wide = jnp.concatenate([factor] * (cw // 128), axis=1)

    for chunk in range(CHUNKS):
        cols = pl.ds(chunk * cw, cw)
        scaled = cot[:, cols].astype(jnp.float32) * gain_ref[:, cols].astype(jnp.float32)
        hid = hidden[:, cols].astype(jnp.float32)
        grad[:, cols] = (inverse_wide * scaled - hid * factor_wide).astype(jnp.bfloat16)

    def p_copy(source, to, part, device):
        cols = pl.ds(part * pw, pw)
        return remote(
            product.at[pl.ds(pl.multiple_of(to * cap, 16), cap), cols],
            returned.at[pl.ds(pl.multiple_of(source * cap, 16), cap), cols],
            p_send.at[part, to], p_recv.at[part, source], device,
        )

    for part in range(PARTS):
        value = lax.dot_general(
            grad[...], weight[pl.ds(part * pw, pw), :], (((1,), (1,)), ((), ())),
            preferred_element_type=jnp.float32,
        )
        product[:, pl.ds(part * pw, pw)] = value.astype(jnp.bfloat16)
        for to in (d_dp, x_dp, y_dp, dp):
            start(p_copy(dp, to, part, (other, to, tp)))

    def r_copy(owner, source, part, k, device):
        cols = pl.ds(part * pw, pw)
        return remote(
            tokens.at[pl.ds(pl.multiple_of(owner * tok_q, 16), tok_q), cols],
            partial.at[source, :, cols],
            r_send.at[part, k], r_recv.at[part, source], device,
        )

    def g_copy(owner, part, k, device):
        ref = result.at[pl.ds(pl.multiple_of(owner * tok_q, 16), tok_q), pl.ds(part * pw, pw)]
        return remote(ref, ref, g_send.at[part, k], g_recv.at[part, owner], device)

    def normalize(chunk):
        cols = pl.ds(chunk * cw, cw)
        hid = hidden[:, cols].astype(jnp.float32)
        normed_ref[:, cols] = (
            hid * inverse_wide * gain_ref[:, cols].astype(jnp.float32)
        ).astype(jnp.bfloat16)

    for chunk in range(CHUNKS // 2):
        normalize(chunk)
    for part in range(PARTS):
        cols = pl.ds(part * pw, pw)
        for source in range(n_dp):
            p_copy(source, source, part, to_sib).wait_recv()
        tokens[:, cols] = jnp.dot(
            unplacer, returned[:, cols], preferred_element_type=jnp.float32
        ).astype(jnp.bfloat16)
        for k in (2, 1, 3):
            to = lax.rem(tp + k, n_tp)
            start(r_copy(to, tp, part, k, (sec, dp, to)))
    for chunk in range(CHUNKS // 2, CHUNKS):
        normalize(chunk)
    mine_rows = pl.ds(pl.multiple_of(tp * tok_q, 16), tok_q)
    for part in range(PARTS):
        cols = pl.ds(part * pw, pw)
        value = tokens[mine_rows, cols].astype(jnp.float32)
        for k in range(1, n_tp):
            who = lax.rem(tp + k, n_tp)
            r_copy(tp, who, part, k, to_sib).wait_recv()
            value = value + partial[who, :, cols].astype(jnp.float32)
        result[mine_rows, cols] = value.astype(jnp.bfloat16)
        for k in (2, 1, 3):
            start(g_copy(tp, part, k, (sec, dp, lax.rem(tp + k, n_tp))))
    for part in range(PARTS):
        for k in range(1, n_tp):
            g_copy(lax.rem(tp + k, n_tp), part, k, to_sib).wait_recv()
    grad_ref[...] = result[...]
    for copy in sent:
        copy.wait_send()


def kernel_body(feats, dest, proj_w, proj_b, text, gain, cot):
    n_dp, n_tp = lax.axis_size("dp"), lax.axis_size("tp")
    per_device, vision = feats.shape[1:]
    rows, width = text.shape[1:]
    quarter = rows // n_dp // n_tp
    bf = jnp.bfloat16
    dma = pltpu.SemaphoreType.DMA
    vmem = pl.BlockSpec(memory_space=pltpu.VMEM)
    hbm = pl.BlockSpec(memory_space=pl.ANY)
    normed, feature_grad = pl.pallas_call(
        kernel,
        out_shape=(
            jax.ShapeDtypeStruct((rows, width), bf),
            jax.ShapeDtypeStruct((per_device, vision), bf),
        ),
        in_specs=[vmem, vmem, hbm, vmem, hbm, vmem, hbm],
        out_specs=(vmem, vmem),
        scratch_shapes=[
            pltpu.VMEM((vision, width), bf),
            pltpu.VMEM((rows, width), bf),
            pltpu.VMEM((rows, width), bf),
            pltpu.VMEM((n_dp, quarter, vision + FLAG), bf),
            pltpu.VMEM((n_dp, n_tp, quarter, vision + FLAG), bf),
            pltpu.VMEM((rows, width), bf),
            pltpu.VMEM((rows, width), bf),
            pltpu.VMEM((rows, vision), bf),
            pltpu.VMEM((rows, vision), bf),
            pltpu.VMEM((per_device, vision), bf),
            pltpu.VMEM((n_tp, per_device // n_tp, vision), bf),
            pltpu.VMEM((per_device, vision), bf),
            pltpu.VMEM((n_tp, 8, rows), jnp.float32),
            dma((3,)),
            dma((CHUNKS, 8)),
            dma((CHUNKS, 8)),
            dma((n_dp,)),
            dma((n_dp,)),
            dma((n_tp,)),
            dma((n_tp,)),
            dma((n_tp,)),
            dma((n_tp,)),
            dma((PARTS, n_dp)),
            dma((PARTS, n_dp)),
            dma((PARTS, n_tp)),
            dma((PARTS, n_tp)),
            dma((PARTS, n_tp)),
            dma((PARTS, n_tp)),
        ],
        compiler_params=pltpu.CompilerParams(
            collective_id=0, has_side_effects=True, vmem_limit_bytes=44 * 1024 * 1024
        ),
    )(
        feats[0], dest[0], proj_w, proj_b.reshape(1, width), text[0], gain.reshape(1, width), cot[0]
    )
    return normed[None], feature_grad[None]


def solution(mesh):
    in_specs = (
        P("sec", "dp", None),
        P("sec", "dp", None),
        P(("sec", "dp"), "tp"),
        P("tp"),
        P("sec", "dp", "tp"),
        P("tp"),
        P("sec", "dp", "tp"),
    )
    out_specs = (P("sec", "dp", "tp"), P("sec", "dp", None))
    small = mesh.shape["sec"] == 2 and mesh.shape["dp"] == 4 and mesh.shape["tp"] == 4
    return jax.shard_map(kernel_body if small else body, mesh=mesh, in_specs=in_specs, out_specs=out_specs, check_vma=False)
```

```python
import functools

import jax
import jax.numpy as jnp
from jax import lax
from jax.experimental import pallas as pl
from jax.experimental.pallas import tpu as pltpu
from jax.sharding import PartitionSpec as P


def from_behind(value, axis, steps):
    count = lax.axis_size(axis)
    pairs = [(source, (source + steps) % count) for source in range(count)]
    return lax.ppermute(value, axis, pairs)


def route_forward(outgoing):
    regrouped = lax.all_to_all(outgoing, "dp", split_axis=0, concat_axis=0, tiled=True)
    return from_behind(regrouped, "sec", 1)


def route_backward(incoming):
    hopped = from_behind(incoming, "sec", -1)
    return lax.all_to_all(hopped, "dp", split_axis=0, concat_axis=0, tiled=True)


def body(feats, dest, proj_w, proj_b, text, gain, cot):
    rows_in = feats[0]
    per_device = rows_in.shape[0]
    group_size = lax.axis_size("dp")
    tp_size = lax.axis_size("tp")
    capacity = 2 * per_device // group_size
    slot_total = group_size * capacity
    weight = lax.all_gather(proj_w, ("sec", "dp"), axis=0, tiled=True)
    target = dest[0, :, 0]
    lanes = jnp.arange(group_size, dtype=jnp.int32)
    onehot = (target[:, None] == lanes[None, :]).astype(jnp.int32)
    before = jnp.cumsum(onehot, axis=0) - onehot
    position = jnp.sum(before * onehot, axis=1)
    slot_index = target * capacity + position
    placer = (jnp.arange(slot_total, dtype=jnp.int32)[:, None] == slot_index[None, :]).astype(
        jnp.bfloat16
    )
    bias_wide = proj_b.astype(jnp.float32)
    counts = jnp.sum(onehot, axis=0).reshape(group_size, 1)
    counts_moved = lax.all_to_all(counts, "dp", split_axis=0, concat_axis=0, tiled=True)
    counts_in = from_behind(counts_moved, "sec", 1)
    occupied = (jnp.arange(capacity, dtype=jnp.int32)[None, :] < counts_in).reshape(slot_total, 1)
    projected = (jnp.dot(rows_in, weight, preferred_element_type=jnp.float32) + bias_wide).astype(
        jnp.bfloat16
    )
    outgoing = jnp.dot(placer, projected, preferred_element_type=jnp.float32).astype(jnp.bfloat16)
    arrived = route_forward(outgoing.reshape(group_size, capacity, -1))
    packed = arrived.reshape(slot_total, -1)
    gain_wide = gain.astype(jnp.float32)
    hidden = jnp.where(occupied, packed.astype(jnp.float32), text[0].astype(jnp.float32))
    scaled = cot[0].astype(jnp.float32) * gain_wide
    squares, cross = lax.psum(
        (jnp.sum(hidden * hidden, axis=1), jnp.sum(scaled * hidden, axis=1)), "tp"
    )
    full_width = hidden.shape[1] * tp_size
    inverse = lax.rsqrt(squares / full_width + 1e-05)
    normed = (hidden * inverse[:, None] * gain_wide).astype(jnp.bfloat16)
    grad_hidden = (
        inverse[:, None] * scaled
        - hidden * (inverse * inverse * inverse * cross / full_width)[:, None]
    ).astype(jnp.bfloat16)
    returned = route_backward(grad_hidden.reshape(group_size, capacity, -1)).reshape(slot_total, -1)
    grad_tokens = jnp.dot(placer.T, returned, preferred_element_type=jnp.float32).astype(
        jnp.bfloat16
    )
    partial_value = lax.dot_general(
        grad_tokens, weight, (((1,), (1,)), ((), ())), preferred_element_type=jnp.float32
    )
    feature_grad = lax.psum(partial_value, "tp").astype(jnp.bfloat16)
    return (normed[None], feature_grad[None])


MESH = pl.DeviceIdType.MESH
FLAG = 128
CHUNKS = 8
AHEAD = 3
PARTS = 5


def kernel(
    feats_hbm, dest_ref, shard_hbm, bias_ref, text_hbm, gain_ref, cot_hbm,
    normed_ref, grad_ref,
    feats, weight, text, cot, outbox, slots, hidden, grad, product, returned, tokens, partial, result, stats,
    local_sem, w_send, w_recv, x_send, x_recv, y_send, y_recv, s_send, s_recv,
    p_send, p_recv, r_send, r_recv, g_send, g_recv,
):
    sec, dp, tp = lax.axis_index("sec"), lax.axis_index("dp"), lax.axis_index("tp")
    other = 1 - sec
    x_dp = dp + 1 - 2 * lax.rem(dp, 2)
    y_dp = lax.rem(dp + 2, 4)
    d_dp = 3 - dp
    per_device, vision = feats.shape
    depth, width = shard_hbm.shape
    n_dp, n_tp, quarter, _ = slots.shape
    cap = n_tp * quarter
    rows = n_dp * cap
    cw = width // CHUNKS
    pw = vision // PARTS
    tok_q = per_device // n_tp
    half = depth // 2

    def block(sec_of, dp_of):
        return pl.multiple_of((sec_of * n_dp + dp_of) * depth, 16)

    own = block(sec, dp)
    in_feats = pltpu.make_async_copy(feats_hbm, feats, local_sem.at[CHUNKS])
    in_text = pltpu.make_async_copy(text_hbm, text, local_sem.at[CHUNKS + 1])
    in_cot = pltpu.make_async_copy(cot_hbm, cot, local_sem.at[CHUNKS + 2])
    in_shard = [
        pltpu.make_async_copy(
            shard_hbm.at[:, pl.ds(chunk * cw, cw)],
            weight.at[chunk, pl.ds(own, depth)],
            local_sem.at[chunk],
        )
        for chunk in range(CHUNKS)
    ]
    for copy in [in_feats, *in_shard, in_text, in_cot]:
        copy.start()

    barrier = pltpu.get_barrier_semaphore()
    peers = [(sec, x_dp, tp), (sec, y_dp, tp), (sec, d_dp, tp)]
    peers += [(other, dp, tp), (other, x_dp, tp), (other, y_dp, tp), (other, d_dp, tp)]
    peers += [(sec, dp, lax.rem(tp + k, n_tp)) for k in range(1, n_tp)]
    for peer in peers:
        pl.semaphore_signal(barrier, inc=1, device_id=peer, device_id_type=MESH)

    def remote(src, dst, send, recv, device):
        return pltpu.make_async_remote_copy(
            src_ref=src, dst_ref=dst, send_sem=send, recv_sem=recv,
            device_id=device, device_id_type=MESH,
        )

    sent = []

    def start(copy):
        copy.start()
        sent.append(copy)

    def w_copy(first, count, chunk, kind, device):
        ref = weight.at[chunk, pl.ds(first, count)]
        return remote(ref, ref, w_send.at[chunk, kind], w_recv.at[chunk, kind], device)

    to_x, to_y, to_sib = (sec, x_dp, tp), (sec, y_dp, tp), (other, dp, tp)
    jx, jy, jd = block(sec, x_dp), block(sec, y_dp), block(sec, d_dp)
    jd_low = pl.multiple_of(jd + half, 16)
    jy_low = pl.multiple_of(jy + half, 16)
    sib = [block(other, k) for k in (dp, x_dp, y_dp, d_dp)]

    def send_own(chunk):
        in_shard[chunk].wait()
        start(w_copy(own, depth, chunk, 0, to_x))
        start(w_copy(own, depth, chunk, 1, to_y))
        start(w_copy(own, depth, chunk, 4, to_sib))

    pl.semaphore_wait(barrier, len(peers))

    send_own(0)
    send_own(1)

    t_row = dest_ref[...].astype(jnp.float32)
    square = (per_device, per_device)
    down = lax.broadcasted_iota(jnp.int32, square, 0)
    along = lax.broadcasted_iota(jnp.int32, square, 1)
    t_col = jnp.sum(jnp.where(down == along, t_row, 0.0), axis=1, keepdims=True)
    same = t_col == t_row
    before_row = jnp.sum(jnp.where(same & (down < along), 1.0, 0.0), axis=0, keepdims=True)
    before_col = jnp.sum(jnp.where(same & (along < down), 1.0, 0.0), axis=1, keepdims=True)
    slot_row = (t_row * cap + before_row).astype(jnp.int32)
    slot_col = (t_col * cap + before_col).astype(jnp.int32)
    mine = lax.broadcasted_iota(jnp.int32, (n_dp * quarter, per_device), 0)
    mine = mine + (mine // quarter) * (cap - quarter) + tp * quarter
    placer = jnp.where(mine == slot_row, 1.0, 0.0)
    filled = jnp.broadcast_to(jnp.sum(placer, axis=1, keepdims=True), (n_dp * quarter, FLAG))
    in_feats.wait()
    routed = jnp.dot(placer.astype(jnp.bfloat16), feats[...], preferred_element_type=jnp.float32)
    outbox[:, :, pl.ds(0, vision)] = routed.astype(jnp.bfloat16).reshape(n_dp, quarter, vision)
    outbox[:, :, pl.ds(vision, FLAG)] = filled.astype(jnp.bfloat16).reshape(n_dp, quarter, FLAG)
    unplacer = jnp.where(
        slot_col == lax.broadcasted_iota(jnp.int32, (per_device, rows), 1), 1.0, 0.0
    ).astype(jnp.bfloat16)

    for to in (d_dp, x_dp, y_dp, dp):
        start(remote(outbox.at[to], slots.at[dp, tp], x_send.at[to], x_recv.at[dp], (other, to, tp)))
    for chunk in range(2, AHEAD):
        send_own(chunk)
    for source in range(n_dp):
        remote(outbox.at[source], slots.at[source, tp], x_send.at[source], x_recv.at[source], to_sib).wait_recv()
    for k in range(1, n_tp):
        to = lax.rem(tp + k, n_tp)
        start(remote(slots.at[:, tp], slots.at[:, tp], y_send.at[k], y_recv.at[tp], (sec, dp, to)))

    def project(chunk, square_sum, cross_sum):
        cols = pl.ds(chunk * cw, cw)
        value = jnp.dot(
            slots[:, :, :, pl.ds(0, vision)].reshape(rows, vision),
            weight[chunk],
            preferred_element_type=jnp.float32,
        )
        value = (value + bias_ref[:, cols].astype(jnp.float32)).astype(jnp.bfloat16)
        flag = slots[:, :, :, pl.ds(vision, FLAG)].reshape(rows, FLAG).astype(jnp.float32)
        flag = jnp.concatenate([flag] * (cw // FLAG), axis=1)
        hid = jnp.where(flag > 0.5, value.astype(jnp.float32), text[:, cols].astype(jnp.float32))
        hidden[:, cols] = hid.astype(jnp.bfloat16)
        scaled = cot[:, cols].astype(jnp.float32) * gain_ref[:, cols].astype(jnp.float32)
        for first in range(0, cw, 128):
            part = hid[:, first:first + 128]
            square_sum = square_sum + part * part
            cross_sum = cross_sum + part * scaled[:, first:first + 128]
        return square_sum, cross_sum

    square_sum = jnp.zeros((rows, 128), jnp.float32)
    cross_sum = jnp.zeros((rows, 128), jnp.float32)
    ready = {
        CHUNKS - 1: range(CHUNKS // 2 - 1),
        CHUNKS: range(CHUNKS // 2 - 1, CHUNKS - 1),
        CHUNKS + 1: (CHUNKS - 1,),
    }
    for step in range(CHUNKS + 2):
        if step < CHUNKS:
            w_copy(jx, depth, step, 0, to_x).wait_recv()
            start(w_copy(jx, half, step, 2, to_y))
            w_copy(jy, depth, step, 1, to_y).wait_recv()
            start(w_copy(jy_low, half, step, 3, to_x))
            start(w_copy(jx, depth, step, 5, to_sib))
            start(w_copy(jy, depth, step, 6, to_sib))
            if step + AHEAD < CHUNKS:
                send_own(step + AHEAD)
        if 1 <= step <= CHUNKS:
            w_copy(jd, half, step - 1, 2, to_y).wait_recv()
            w_copy(jd_low, half, step - 1, 3, to_x).wait_recv()
            start(w_copy(jd, depth, step - 1, 7, to_sib))
        if step == CHUNKS - 1:
            for k in range(1, n_tp):
                who = lax.rem(tp + k, n_tp)
                remote(slots.at[:, who], slots.at[:, who], y_send.at[k], y_recv.at[who], to_sib).wait_recv()
            in_text.wait()
            in_cot.wait()
        for chunk in ready.get(step, ()):
            for kind in range(4):
                w_copy(sib[kind], depth, chunk, 4 + kind, to_sib).wait_recv()
            square_sum, cross_sum = project(chunk, square_sum, cross_sum)

    stats[tp, pl.ds(0, 1), :] = jnp.sum(square_sum.T, axis=0, keepdims=True)
    stats[tp, pl.ds(1, 1), :] = jnp.sum(cross_sum.T, axis=0, keepdims=True)
    for k in range(1, n_tp):
        to = lax.rem(tp + k, n_tp)
        start(remote(stats.at[tp], stats.at[tp], s_send.at[k], s_recv.at[tp], (sec, dp, to)))
    for k in range(1, n_tp):
        who = lax.rem(tp + k, n_tp)
        remote(stats.at[who], stats.at[who], s_send.at[k], s_recv.at[who], to_sib).wait_recv()
    total = stats[0] + stats[1] + stats[2] + stats[3]
    full_width = width * n_tp
    inverse = lax.rsqrt(total[0:1] / full_width + 1e-05)
    factor = inverse * inverse * inverse * total[1:2] / full_width
    inverse = jnp.broadcast_to(inverse, (128, rows)).T
    factor = jnp.broadcast_to(factor, (128, rows)).T
    inverse_wide = jnp.concatenate([inverse] * (cw // 128), axis=1)
    factor_wide = jnp.concatenate([factor] * (cw // 128), axis=1)

    for chunk in range(CHUNKS):
        cols = pl.ds(chunk * cw, cw)
        scaled = cot[:, cols].astype(jnp.float32) * gain_ref[:, cols].astype(jnp.float32)
        hid = hidden[:, cols].astype(jnp.float32)
        grad[:, cols] = (inverse_wide * scaled - hid * factor_wide).astype(jnp.bfloat16)

    def p_copy(source, to, part, device):
        return remote(
            product.at[part, pl.ds(pl.multiple_of(to * cap, 16), cap)],
            returned.at[part, pl.ds(pl.multiple_of(source * cap, 16), cap)],
            p_send.at[part, to], p_recv.at[part, source], device,
        )

    for part in range(PARTS):
        value = jnp.zeros((rows, pw), jnp.float32)
        for chunk in range(CHUNKS):
            value = value + lax.dot_general(
                grad[:, pl.ds(chunk * cw, cw)], weight[chunk, pl.ds(part * pw, pw), :],
                (((1,), (1,)), ((), ())), preferred_element_type=jnp.float32,
            )
        product[part] = value.astype(jnp.bfloat16)
        for to in (d_dp, x_dp, y_dp, dp):
            start(p_copy(dp, to, part, (other, to, tp)))

    def r_copy(owner, source, part, k, device):
        return remote(
            tokens.at[part, pl.ds(pl.multiple_of(owner * tok_q, 16), tok_q)],
            partial.at[part, source],
            r_send.at[part, k], r_recv.at[part, source], device,
        )

    def g_copy(owner, part, k, device):
        ref = result.at[part, pl.ds(pl.multiple_of(owner * tok_q, 16), tok_q)]
        return remote(ref, ref, g_send.at[part, k], g_recv.at[part, owner], device)

    def normalize(chunk):
        cols = pl.ds(chunk * cw, cw)
        hid = hidden[:, cols].astype(jnp.float32)
        normed_ref[:, cols] = (
            hid * inverse_wide * gain_ref[:, cols].astype(jnp.float32)
        ).astype(jnp.bfloat16)

    for chunk in range(CHUNKS // 2):
        normalize(chunk)
    for part in range(PARTS):
        for source in range(n_dp):
            p_copy(source, source, part, to_sib).wait_recv()
        tokens[part] = jnp.dot(
            unplacer, returned[part], preferred_element_type=jnp.float32
        ).astype(jnp.bfloat16)
        for k in (2, 1, 3):
            to = lax.rem(tp + k, n_tp)
            start(r_copy(to, tp, part, k, (sec, dp, to)))
    for chunk in range(CHUNKS // 2, CHUNKS):
        normalize(chunk)
    mine_rows = pl.ds(pl.multiple_of(tp * tok_q, 16), tok_q)
    for part in range(PARTS):
        value = tokens[part, mine_rows].astype(jnp.float32)
        for k in range(1, n_tp):
            who = lax.rem(tp + k, n_tp)
            r_copy(tp, who, part, k, to_sib).wait_recv()
            value = value + partial[part, who].astype(jnp.float32)
        result[part, mine_rows] = value.astype(jnp.bfloat16)
        for k in (2, 1, 3):
            start(g_copy(tp, part, k, (sec, dp, lax.rem(tp + k, n_tp))))
    for part in range(PARTS):
        for k in range(1, n_tp):
            g_copy(lax.rem(tp + k, n_tp), part, k, to_sib).wait_recv()
        grad_ref[:, pl.ds(part * pw, pw)] = result[part]
    for copy in sent:
        copy.wait_send()


def kernel_body(feats, dest, proj_w, proj_b, text, gain, cot):
    n_dp, n_tp = lax.axis_size("dp"), lax.axis_size("tp")
    per_device, vision = feats.shape[1:]
    rows, width = text.shape[1:]
    quarter = rows // n_dp // n_tp
    bf = jnp.bfloat16
    dma = pltpu.SemaphoreType.DMA
    vmem = pl.BlockSpec(memory_space=pltpu.VMEM)
    hbm = pl.BlockSpec(memory_space=pltpu.HBM)
    normed, feature_grad = pl.pallas_call(
        kernel,
        out_shape=(
            jax.ShapeDtypeStruct((rows, width), bf),
            jax.ShapeDtypeStruct((per_device, vision), bf),
        ),
        in_specs=[hbm, vmem, hbm, vmem, hbm, vmem, hbm],
        out_specs=(vmem, vmem),
        scratch_shapes=[
            pltpu.VMEM((per_device, vision), bf),
            pltpu.VMEM((CHUNKS, vision, width // CHUNKS), bf),
            pltpu.VMEM((rows, width), bf),
            pltpu.VMEM((rows, width), bf),
            pltpu.VMEM((n_dp, quarter, vision + FLAG), bf),
            pltpu.VMEM((n_dp, n_tp, quarter, vision + FLAG), bf),
            pltpu.VMEM((rows, width), bf),
            pltpu.VMEM((rows, width), bf),
            pltpu.VMEM((PARTS, rows, vision // PARTS), bf),
            pltpu.VMEM((PARTS, rows, vision // PARTS), bf),
            pltpu.VMEM((PARTS, per_device, vision // PARTS), bf),
            pltpu.VMEM((PARTS, n_tp, per_device // n_tp, vision // PARTS), bf),
            pltpu.VMEM((PARTS, per_device, vision // PARTS), bf),
            pltpu.VMEM((n_tp, 8, rows), jnp.float32),
            dma((CHUNKS + 3,)),
            dma((CHUNKS, 8)),
            dma((CHUNKS, 8)),
            dma((n_dp,)),
            dma((n_dp,)),
            dma((n_tp,)),
            dma((n_tp,)),
            dma((n_tp,)),
            dma((n_tp,)),
            dma((PARTS, n_dp)),
            dma((PARTS, n_dp)),
            dma((PARTS, n_tp)),
            dma((PARTS, n_tp)),
            dma((PARTS, n_tp)),
            dma((PARTS, n_tp)),
        ],
        compiler_params=pltpu.CompilerParams(
            collective_id=0, has_side_effects=True, vmem_limit_bytes=63 * 1024 * 1024
        ),
    )(
        feats[0], dest.reshape(1, per_device), proj_w, proj_b.reshape(1, width), text[0], gain.reshape(1, width), cot[0]
    )
    return normed[None], feature_grad[None]


def solution(mesh):
    in_specs = (
        P("sec", "dp", None),
        P("sec", "dp", None),
        P(("sec", "dp"), "tp"),
        P("tp"),
        P("sec", "dp", "tp"),
        P("tp"),
        P("sec", "dp", "tp"),
    )
    out_specs = (P("sec", "dp", "tp"), P("sec", "dp", None))
    small = mesh.shape["sec"] == 2 and mesh.shape["dp"] == 4 and mesh.shape["tp"] == 4
    return jax.shard_map(kernel_body if small else body, mesh=mesh, in_specs=in_specs, out_specs=out_specs, check_vma=False)
```

```python
import functools

import jax
import jax.numpy as jnp
from jax import lax
from jax.experimental import pallas as pl
from jax.experimental.pallas import tpu as pltpu
from jax.sharding import PartitionSpec as P


def from_behind(value, axis, steps):
    count = lax.axis_size(axis)
    pairs = [(source, (source + steps) % count) for source in range(count)]
    return lax.ppermute(value, axis, pairs)


def route_forward(outgoing):
    regrouped = lax.all_to_all(outgoing, "dp", split_axis=0, concat_axis=0, tiled=True)
    return from_behind(regrouped, "sec", 1)


def route_backward(incoming):
    hopped = from_behind(incoming, "sec", -1)
    return lax.all_to_all(hopped, "dp", split_axis=0, concat_axis=0, tiled=True)


def body(feats, dest, proj_w, proj_b, text, gain, cot):
    rows_in = feats[0]
    per_device = rows_in.shape[0]
    group_size = lax.axis_size("dp")
    tp_size = lax.axis_size("tp")
    capacity = 2 * per_device // group_size
    slot_total = group_size * capacity
    weight = lax.all_gather(proj_w, ("sec", "dp"), axis=0, tiled=True)
    target = dest[0, :, 0]
    lanes = jnp.arange(group_size, dtype=jnp.int32)
    onehot = (target[:, None] == lanes[None, :]).astype(jnp.int32)
    before = jnp.cumsum(onehot, axis=0) - onehot
    position = jnp.sum(before * onehot, axis=1)
    slot_index = target * capacity + position
    placer = (jnp.arange(slot_total, dtype=jnp.int32)[:, None] == slot_index[None, :]).astype(
        jnp.bfloat16
    )
    bias_wide = proj_b.astype(jnp.float32)
    counts = jnp.sum(onehot, axis=0).reshape(group_size, 1)
    counts_moved = lax.all_to_all(counts, "dp", split_axis=0, concat_axis=0, tiled=True)
    counts_in = from_behind(counts_moved, "sec", 1)
    occupied = (jnp.arange(capacity, dtype=jnp.int32)[None, :] < counts_in).reshape(slot_total, 1)
    projected = (jnp.dot(rows_in, weight, preferred_element_type=jnp.float32) + bias_wide).astype(
        jnp.bfloat16
    )
    outgoing = jnp.dot(placer, projected, preferred_element_type=jnp.float32).astype(jnp.bfloat16)
    arrived = route_forward(outgoing.reshape(group_size, capacity, -1))
    packed = arrived.reshape(slot_total, -1)
    gain_wide = gain.astype(jnp.float32)
    hidden = jnp.where(occupied, packed.astype(jnp.float32), text[0].astype(jnp.float32))
    scaled = cot[0].astype(jnp.float32) * gain_wide
    squares, cross = lax.psum(
        (jnp.sum(hidden * hidden, axis=1), jnp.sum(scaled * hidden, axis=1)), "tp"
    )
    full_width = hidden.shape[1] * tp_size
    inverse = lax.rsqrt(squares / full_width + 1e-05)
    normed = (hidden * inverse[:, None] * gain_wide).astype(jnp.bfloat16)
    grad_hidden = (
        inverse[:, None] * scaled
        - hidden * (inverse * inverse * inverse * cross / full_width)[:, None]
    ).astype(jnp.bfloat16)
    returned = route_backward(grad_hidden.reshape(group_size, capacity, -1)).reshape(slot_total, -1)
    grad_tokens = jnp.dot(placer.T, returned, preferred_element_type=jnp.float32).astype(
        jnp.bfloat16
    )
    partial_value = lax.dot_general(
        grad_tokens, weight, (((1,), (1,)), ((), ())), preferred_element_type=jnp.float32
    )
    feature_grad = lax.psum(partial_value, "tp").astype(jnp.bfloat16)
    return (normed[None], feature_grad[None])


MESH = pl.DeviceIdType.MESH
FLAG = 128
CHUNKS = 8
AHEAD = 3
PARTS = 5


def kernel(
    feats_hbm, dest_ref, shard_hbm, bias_ref, text_hbm, gain_ref, cot_hbm,
    normed_ref, grad_ref,
    feats, weight, text, cot, outbox, slots, hidden, grad, product, returned, tokens, partial, result, stats,
    local_sem, w_send, w_recv, x_send, x_recv, y_send, y_recv, s_send, s_recv,
    p_send, p_recv, r_send, r_recv, g_send, g_recv,
):
    sec, dp, tp = lax.axis_index("sec"), lax.axis_index("dp"), lax.axis_index("tp")
    other = 1 - sec
    x_dp = dp + 1 - 2 * lax.rem(dp, 2)
    y_dp = lax.rem(dp + 2, 4)
    d_dp = 3 - dp
    per_device, vision = feats.shape
    depth, width = shard_hbm.shape
    n_dp, n_tp, quarter, _ = slots.shape
    cap = n_tp * quarter
    rows = n_dp * cap
    cw = width // CHUNKS
    pw = vision // PARTS
    tok_q = per_device // n_tp
    half = depth // 2

    def block(sec_of, dp_of):
        return pl.multiple_of((sec_of * n_dp + dp_of) * depth, 16)

    own = block(sec, dp)
    in_feats = pltpu.make_async_copy(feats_hbm, feats, local_sem.at[CHUNKS])
    in_text = pltpu.make_async_copy(text_hbm, text, local_sem.at[CHUNKS + 1])
    in_cot = pltpu.make_async_copy(cot_hbm, cot, local_sem.at[CHUNKS + 2])
    in_shard = [
        pltpu.make_async_copy(
            shard_hbm.at[:, pl.ds(chunk * cw, cw)],
            weight.at[chunk, pl.ds(own, depth)],
            local_sem.at[chunk],
        )
        for chunk in range(CHUNKS)
    ]
    for copy in [in_feats, *in_shard, in_text, in_cot]:
        copy.start()

    barrier = pltpu.get_barrier_semaphore()
    peers = [(sec, x_dp, tp), (sec, y_dp, tp), (sec, d_dp, tp)]
    peers += [(other, dp, tp), (other, x_dp, tp), (other, y_dp, tp), (other, d_dp, tp)]
    peers += [(sec, dp, lax.rem(tp + k, n_tp)) for k in range(1, n_tp)]
    for peer in peers:
        pl.semaphore_signal(barrier, inc=1, device_id=peer, device_id_type=MESH)

    def remote(src, dst, send, recv, device):
        return pltpu.make_async_remote_copy(
            src_ref=src, dst_ref=dst, send_sem=send, recv_sem=recv,
            device_id=device, device_id_type=MESH,
        )

    sent = []

    def start(copy):
        copy.start()
        sent.append(copy)

    def w_copy(first, count, chunk, kind, device):
        ref = weight.at[chunk, pl.ds(first, count)]
        return remote(ref, ref, w_send.at[chunk, kind], w_recv.at[chunk, kind], device)

    to_x, to_y, to_sib = (sec, x_dp, tp), (sec, y_dp, tp), (other, dp, tp)
    jx, jy, jd = block(sec, x_dp), block(sec, y_dp), block(sec, d_dp)
    jd_low = pl.multiple_of(jd + half, 16)
    jy_low = pl.multiple_of(jy + half, 16)
    sib = [block(other, k) for k in (dp, x_dp, y_dp, d_dp)]

    def send_own(chunk):
        in_shard[chunk].wait()
        start(w_copy(own, depth, chunk, 0, to_x))
        start(w_copy(own, depth, chunk, 1, to_y))
        start(w_copy(own, depth, chunk, 4, to_sib))

    pl.semaphore_wait(barrier, len(peers))

    send_own(0)
    send_own(1)

    t_row = dest_ref[...].astype(jnp.float32)
    square = (per_device, per_device)
    down = lax.broadcasted_iota(jnp.int32, square, 0)
    along = lax.broadcasted_iota(jnp.int32, square, 1)
    t_col = jnp.sum(jnp.where(down == along, t_row, 0.0), axis=1, keepdims=True)
    same = t_col == t_row
    before_row = jnp.sum(jnp.where(same & (down < along), 1.0, 0.0), axis=0, keepdims=True)
    before_col = jnp.sum(jnp.where(same & (along < down), 1.0, 0.0), axis=1, keepdims=True)
    slot_row = (t_row * cap + before_row).astype(jnp.int32)
    slot_col = (t_col * cap + before_col).astype(jnp.int32)
    mine = lax.broadcasted_iota(jnp.int32, (n_dp * quarter, per_device), 0)
    mine = mine + (mine // quarter) * (cap - quarter) + tp * quarter
    placer = jnp.where(mine == slot_row, 1.0, 0.0)
    filled = jnp.broadcast_to(jnp.sum(placer, axis=1, keepdims=True), (n_dp * quarter, FLAG))
    in_feats.wait()
    routed = jnp.dot(placer.astype(jnp.bfloat16), feats[...], preferred_element_type=jnp.float32)
    outbox[:, :, pl.ds(0, vision)] = routed.astype(jnp.bfloat16).reshape(n_dp, quarter, vision)
    outbox[:, :, pl.ds(vision, FLAG)] = filled.astype(jnp.bfloat16).reshape(n_dp, quarter, FLAG)
    unplacer = jnp.where(
        slot_col == lax.broadcasted_iota(jnp.int32, (per_device, rows), 1), 1.0, 0.0
    ).astype(jnp.bfloat16)

    for to in (d_dp, x_dp, y_dp, dp):
        start(remote(outbox.at[to], slots.at[dp, tp], x_send.at[to], x_recv.at[dp], (other, to, tp)))
    for chunk in range(2, AHEAD):
        send_own(chunk)
    for source in range(n_dp):
        remote(outbox.at[source], slots.at[source, tp], x_send.at[source], x_recv.at[source], to_sib).wait_recv()
    for k in range(1, n_tp):
        to = lax.rem(tp + k, n_tp)
        start(remote(slots.at[:, tp], slots.at[:, tp], y_send.at[k], y_recv.at[tp], (sec, dp, to)))

    def project(chunk, square_sum, cross_sum):
        cols = pl.ds(chunk * cw, cw)
        value = jnp.dot(
            slots[:, :, :, pl.ds(0, vision)].reshape(rows, vision),
            weight[chunk],
            preferred_element_type=jnp.float32,
        )
        value = (value + bias_ref[cols].astype(jnp.float32).reshape(1, cw)).astype(jnp.bfloat16)
        flag = slots[:, :, :, pl.ds(vision, FLAG)].reshape(rows, FLAG).astype(jnp.float32)
        flag = jnp.concatenate([flag] * (cw // FLAG), axis=1)
        hid = jnp.where(flag > 0.5, value.astype(jnp.float32), text[:, cols].astype(jnp.float32))
        hidden[:, cols] = hid.astype(jnp.bfloat16)
        scaled = cot[:, cols].astype(jnp.float32) * gain_ref[cols].astype(jnp.float32).reshape(1, cw)
        for first in range(0, cw, 128):
            part = hid[:, first:first + 128]
            square_sum = square_sum + part * part
            cross_sum = cross_sum + part * scaled[:, first:first + 128]
        return square_sum, cross_sum

    square_sum = jnp.zeros((rows, 128), jnp.float32)
    cross_sum = jnp.zeros((rows, 128), jnp.float32)
    ready = {
        CHUNKS - 1: range(CHUNKS // 2 - 1),
        CHUNKS: range(CHUNKS // 2 - 1, CHUNKS - 1),
        CHUNKS + 1: (CHUNKS - 1,),
    }
    for step in range(CHUNKS + 2):
        if step < CHUNKS:
            w_copy(jx, depth, step, 0, to_x).wait_recv()
            start(w_copy(jx, half, step, 2, to_y))
            w_copy(jy, depth, step, 1, to_y).wait_recv()
            start(w_copy(jy_low, half, step, 3, to_x))
            start(w_copy(jx, depth, step, 5, to_sib))
            start(w_copy(jy, depth, step, 6, to_sib))
            if step + AHEAD < CHUNKS:
                send_own(step + AHEAD)
        if 1 <= step <= CHUNKS:
            w_copy(jd, half, step - 1, 2, to_y).wait_recv()
            w_copy(jd_low, half, step - 1, 3, to_x).wait_recv()
            start(w_copy(jd, depth, step - 1, 7, to_sib))
        if step == CHUNKS - 1:
            for k in range(1, n_tp):
                who = lax.rem(tp + k, n_tp)
                remote(slots.at[:, who], slots.at[:, who], y_send.at[k], y_recv.at[who], to_sib).wait_recv()
            in_text.wait()
            in_cot.wait()
        for chunk in ready.get(step, ()):
            for kind in range(4):
                w_copy(sib[kind], depth, chunk, 4 + kind, to_sib).wait_recv()
            square_sum, cross_sum = project(chunk, square_sum, cross_sum)

    stats[tp, pl.ds(0, 1), :] = jnp.sum(square_sum.T, axis=0, keepdims=True)
    stats[tp, pl.ds(1, 1), :] = jnp.sum(cross_sum.T, axis=0, keepdims=True)
    for k in range(1, n_tp):
        to = lax.rem(tp + k, n_tp)
        start(remote(stats.at[tp], stats.at[tp], s_send.at[k], s_recv.at[tp], (sec, dp, to)))
    for k in range(1, n_tp):
        who = lax.rem(tp + k, n_tp)
        remote(stats.at[who], stats.at[who], s_send.at[k], s_recv.at[who], to_sib).wait_recv()
    total = stats[0] + stats[1] + stats[2] + stats[3]
    full_width = width * n_tp
    inverse = lax.rsqrt(total[0:1] / full_width + 1e-05)
    factor = inverse * inverse * inverse * total[1:2] / full_width
    inverse = jnp.broadcast_to(inverse, (128, rows)).T
    factor = jnp.broadcast_to(factor, (128, rows)).T
    inverse_wide = jnp.concatenate([inverse] * (cw // 128), axis=1)
    factor_wide = jnp.concatenate([factor] * (cw // 128), axis=1)

    for chunk in range(CHUNKS):
        cols = pl.ds(chunk * cw, cw)
        scaled = cot[:, cols].astype(jnp.float32) * gain_ref[cols].astype(jnp.float32).reshape(1, cw)
        hid = hidden[:, cols].astype(jnp.float32)
        grad[:, cols] = (inverse_wide * scaled - hid * factor_wide).astype(jnp.bfloat16)

    def p_copy(source, to, part, device):
        return remote(
            product.at[part, pl.ds(pl.multiple_of(to * cap, 16), cap)],
            returned.at[part, pl.ds(pl.multiple_of(source * cap, 16), cap)],
            p_send.at[part, to], p_recv.at[part, source], device,
        )

    for part in range(PARTS):
        value = jnp.zeros((rows, pw), jnp.float32)
        for chunk in range(CHUNKS):
            value = value + lax.dot_general(
                grad[:, pl.ds(chunk * cw, cw)], weight[chunk, pl.ds(part * pw, pw), :],
                (((1,), (1,)), ((), ())), preferred_element_type=jnp.float32,
            )
        product[part] = value.astype(jnp.bfloat16)
        for to in (d_dp, x_dp, y_dp, dp):
            start(p_copy(dp, to, part, (other, to, tp)))

    def r_copy(owner, source, part, k, device):
        return remote(
            tokens.at[part, pl.ds(pl.multiple_of(owner * tok_q, 16), tok_q)],
            partial.at[part, source],
            r_send.at[part, k], r_recv.at[part, source], device,
        )

    def g_copy(owner, part, k, device):
        ref = result.at[part, pl.ds(pl.multiple_of(owner * tok_q, 16), tok_q)]
        return remote(ref, ref, g_send.at[part, k], g_recv.at[part, owner], device)

    def normalize(chunk):
        cols = pl.ds(chunk * cw, cw)
        hid = hidden[:, cols].astype(jnp.float32)
        normed_ref[:, cols] = (
            hid * inverse_wide * gain_ref[cols].astype(jnp.float32).reshape(1, cw)
        ).astype(jnp.bfloat16)

    for chunk in range(CHUNKS // 2):
        normalize(chunk)
    for part in range(PARTS):
        for source in range(n_dp):
            p_copy(source, source, part, to_sib).wait_recv()
        tokens[part] = jnp.dot(
            unplacer, returned[part], preferred_element_type=jnp.float32
        ).astype(jnp.bfloat16)
        for k in (2, 1, 3):
            to = lax.rem(tp + k, n_tp)
            start(r_copy(to, tp, part, k, (sec, dp, to)))
    for chunk in range(CHUNKS // 2, CHUNKS):
        normalize(chunk)
    mine_rows = pl.ds(pl.multiple_of(tp * tok_q, 16), tok_q)
    for part in range(PARTS):
        value = tokens[part, mine_rows].astype(jnp.float32)
        for k in range(1, n_tp):
            who = lax.rem(tp + k, n_tp)
            r_copy(tp, who, part, k, to_sib).wait_recv()
            value = value + partial[part, who].astype(jnp.float32)
        result[part, mine_rows] = value.astype(jnp.bfloat16)
        for k in (2, 1, 3):
            start(g_copy(tp, part, k, (sec, dp, lax.rem(tp + k, n_tp))))
    for part in range(PARTS):
        for k in range(1, n_tp):
            g_copy(lax.rem(tp + k, n_tp), part, k, to_sib).wait_recv()
        grad_ref[:, pl.ds(part * pw, pw)] = result[part]
    for copy in sent:
        copy.wait_send()


def kernel_body(feats, dest, proj_w, proj_b, text, gain, cot):
    n_dp, n_tp = lax.axis_size("dp"), lax.axis_size("tp")
    per_device, vision = feats.shape[1:]
    rows, width = text.shape[1:]
    quarter = rows // n_dp // n_tp
    bf = jnp.bfloat16
    dma = pltpu.SemaphoreType.DMA
    vmem = pl.BlockSpec(memory_space=pltpu.VMEM)
    hbm = pl.BlockSpec(memory_space=pltpu.HBM)
    normed, feature_grad = pl.pallas_call(
        kernel,
        out_shape=(
            jax.ShapeDtypeStruct((rows, width), bf),
            jax.ShapeDtypeStruct((per_device, vision), bf),
        ),
        in_specs=[hbm, vmem, hbm, vmem, hbm, vmem, hbm],
        out_specs=(vmem, vmem),
        scratch_shapes=[
            pltpu.VMEM((per_device, vision), bf),
            pltpu.VMEM((CHUNKS, vision, width // CHUNKS), bf),
            pltpu.VMEM((rows, width), bf),
            pltpu.VMEM((rows, width), bf),
            pltpu.VMEM((n_dp, quarter, vision + FLAG), bf),
            pltpu.VMEM((n_dp, n_tp, quarter, vision + FLAG), bf),
            pltpu.VMEM((rows, width), bf),
            pltpu.VMEM((rows, width), bf),
            pltpu.VMEM((PARTS, rows, vision // PARTS), bf),
            pltpu.VMEM((PARTS, rows, vision // PARTS), bf),
            pltpu.VMEM((PARTS, per_device, vision // PARTS), bf),
            pltpu.VMEM((PARTS, n_tp, per_device // n_tp, vision // PARTS), bf),
            pltpu.VMEM((PARTS, per_device, vision // PARTS), bf),
            pltpu.VMEM((n_tp, 8, rows), jnp.float32),
            dma((CHUNKS + 3,)),
            dma((CHUNKS, 8)),
            dma((CHUNKS, 8)),
            dma((n_dp,)),
            dma((n_dp,)),
            dma((n_tp,)),
            dma((n_tp,)),
            dma((n_tp,)),
            dma((n_tp,)),
            dma((PARTS, n_dp)),
            dma((PARTS, n_dp)),
            dma((PARTS, n_tp)),
            dma((PARTS, n_tp)),
            dma((PARTS, n_tp)),
            dma((PARTS, n_tp)),
        ],
        compiler_params=pltpu.CompilerParams(
            collective_id=0, has_side_effects=True, vmem_limit_bytes=63 * 1024 * 1024
        ),
    )(
        feats[0], dest.reshape(1, per_device), proj_w, proj_b, text[0], gain, cot[0]
    )
    return normed[None], feature_grad[None]


def solution(mesh):
    in_specs = (
        P("sec", "dp", None),
        P("sec", "dp", None),
        P(("sec", "dp"), "tp"),
        P("tp"),
        P("sec", "dp", "tp"),
        P("tp"),
        P("sec", "dp", "tp"),
    )
    out_specs = (P("sec", "dp", "tp"), P("sec", "dp", None))
    small = mesh.shape["sec"] == 2 and mesh.shape["dp"] == 4 and mesh.shape["tp"] == 4
    return jax.shard_map(kernel_body if small else body, mesh=mesh, in_specs=in_specs, out_specs=out_specs, check_vma=False)
```
